32 devices in a mesh: ens: 4 (over y, core), trc: 8 (over z, x).
Axes of the slice: x: 2, y: 2, z: 4, core: 2. Of those that a mesh axis runs over, the one named last changes fastest.
Arguments:
- tracer_state: bfloat16 [1536, 4, 8, 1440], P(('ens', 'trc')), may hold values from -6 to 6
- velocity: float32 [2, 4, 8, 1440], replicated, may hold values from -0.24 to 0.24
- land_mask: int32 [8, 1440], replicated, may hold values from 0 to 1, as said below
- in_weight: bfloat16 [24, 256], replicated, may hold values from -1.25 to 1.25
- bias_one: float32 [256], replicated, may hold values from -3 to 3
- hid_weight: bfloat16 [256, 256], replicated, may hold values from -0.375 to 0.375
- bias_two: float32 [256], replicated, may hold values from -3 to 3
- out_coef: float32 [64, 24, 256], P('ens'), may hold values from -6 to 6
- obs_cell: int32 [8, 128], P('trc'), may hold values from 0 to 5759, as said below
- obs_count: int32 [8], P('trc'), may hold values from 16 to 128, as said below
- obs_value: float32 [8, 6, 128], P('trc'), may hold values from -6 to 6
- obs_var: float32 [8, 6, 128], P('trc'), may hold values from 0.05 to 0.5
- obs_noise: float32 [64, 8, 6, 128], P(None, 'trc'), may hold values from -2 to 2
Outputs:
- new_state: bfloat16 [1536, 4, 8, 1440], P('ens', None, 'trc')
- new_coef: float32 [64, 24, 256], P('ens')
The draws below stay inside these ranges and needn't reach their ends.
Inputs may be any that keep to these rules, and one draw needn't show every extreme that they name: `land_mask`: every block of 1 latitude rows (rows k * 1 to (k + 1) - 1) holds at most 1152 ocean columns, and some block exactly 1152. `obs_cell`: every slot names an ocean cell of its block. `obs_count`: some block uses all 128 slots.
All inputs are finite; a program needn't handle non-finite values.
Results may differ from the reference program's by a relative error of at most 0.0068.
Values may be sent and summed in bfloat16 or wider, within the bound.
A program may use at most 128 MiB of HBM per device.

```python
import math
import jax
import jax.numpy as jnp
from jax import lax

NTR = 24
HID = 256
OBS_TR = 6
LON = 1440
ROW_OCEAN = 1152
ADV_STEPS = 2
OBS_CAP = 128
LEV = 4
ROWBLK = 1
MEMBERS = 64
LATS = 8
BLOCKS = 8
COL_DEV = 1440


def land_layout(seed_key):
    key_count, key_block, key_start = jax.random.split(seed_key, 3)
    counts = jax.random.randint(key_count, (LATS,), ROW_OCEAN // 2, ROW_OCEAN + 1)
    full_block = jax.random.randint(key_block, (), 0, LATS // ROWBLK)
    row_block_ids = jnp.arange(LATS) // ROWBLK
    counts = jnp.where(row_block_ids == full_block, ROW_OCEAN, counts)
    starts = jax.random.randint(key_start, (LATS,), 0, LON)
    return (counts, starts)


def draw_land_mask(key, part):
    counts, starts = land_layout(jax.random.fold_in(key, 11))
    longitude = jnp.arange(LON)
    offset = (longitude[None, :] - starts[:, None]) % LON
    return (offset >= LON - counts[:, None]).astype(jnp.int32)


def draw_obs_cell(key, part):
    counts, starts = land_layout(jax.random.fold_in(key, 11))
    key_row, key_level, key_pos = jax.random.split(jax.random.fold_in(key, 23), 3)
    block_count = LATS // ROWBLK
    row_within = jax.random.randint(key_row, (block_count, OBS_CAP), 0, ROWBLK)
    latitude = jnp.arange(block_count)[:, None] * ROWBLK + row_within
    level_ids = jax.random.randint(key_level, (block_count, OBS_CAP), 0, LEV)
    row_counts = counts[latitude]
    ocean_pos = jax.random.randint(key_pos, (block_count, OBS_CAP), 0, row_counts)
    longitude = (starts[latitude] + LON - row_counts + ocean_pos) % LON
    return (level_ids * (ROWBLK * LON) + row_within * LON + longitude).astype(jnp.int32)


def draw_obs_count(key, part):
    key_count, key_full = jax.random.split(jax.random.fold_in(key, 37))
    block_count = LATS // ROWBLK
    counts = jax.random.randint(key_count, (block_count,), OBS_CAP // 8, OBS_CAP // 2 + 1)
    full_block = jax.random.randint(key_full, (), 0, block_count)
    return jnp.where(jnp.arange(block_count) == full_block, OBS_CAP, counts).astype(jnp.int32)


def shard_levels(stream_key, dims, cuts, least, largest):
    loudness = 1.0
    for position, blocks in cuts:
        heights = jax.random.uniform(jax.random.fold_in(jax.random.fold_in(stream_key, 6), position), (blocks,), jnp.float32, least / len(cuts), largest / len(cuts))
        loudness = loudness * jnp.repeat(jnp.exp(heights), dims[position] // blocks).reshape((-1,) + (1,) * (len(dims) - 1 - position))
    return loudness


def bell_draw(own_key, shape, scale, most, pieces=(), held_as=jnp.bfloat16):
    result = scale * jax.random.normal(own_key, shape, jnp.float32)
    if pieces:
        result = result * shard_levels(own_key, shape, pieces, -0.22, 0.18)
    return jnp.clip(result, -most, most).astype(held_as)


def setup_inputs(seed: int = 0) -> dict:
    seeds = jax.random.split(jax.random.key(seed), 14)
    tracer_state = bell_draw(seeds[0], (MEMBERS * NTR, LEV, LATS, LON), 1.0, 6.0, ((0, 32),))
    velocity = jnp.clip(jax.random.uniform(seeds[1], (2, LEV, LATS, LON), jnp.float32, -0.24, 0.24), -0.24, 0.24)
    land_mask = draw_land_mask(jax.random.fold_in(seeds[13], 71), 0)
    in_weight = bell_draw(seeds[3], (NTR, HID), NTR ** -0.5, 1.25)
    bias_one = bell_draw(seeds[4], (HID,), 0.5, 3.0, (), jnp.float32)
    hid_weight = bell_draw(seeds[5], (HID, HID), HID ** -0.5, 0.375)
    bias_two = bell_draw(seeds[6], (HID,), 0.5, 3.0, (), jnp.float32)
    out_coef = bell_draw(seeds[7], (MEMBERS, NTR, HID), 1.0, 6.0, ((0, 4),), jnp.float32)
    obs_cell = draw_obs_cell(jax.random.fold_in(seeds[13], 71), 0)
    obs_count = draw_obs_count(jax.random.fold_in(seeds[13], 71), 0)
    obs_value = bell_draw(seeds[10], (BLOCKS, OBS_TR, OBS_CAP), 1.0, 6.0, ((0, 8),), jnp.float32)
    obs_var = jnp.clip(jnp.exp(math.log(0.5) - 2.3025851 * jax.random.uniform(seeds[11], (BLOCKS, OBS_TR, OBS_CAP), jnp.float32) ** shard_levels(seeds[11], (BLOCKS, OBS_TR, OBS_CAP), ((0, 8),), -0.2, 0.2)), 0.05, 0.5)
    obs_noise = bell_draw(seeds[12], (MEMBERS, BLOCKS, OBS_TR, OBS_CAP), 0.3, 2.0, ((1, 8),), jnp.float32)
    return dict(tracer_state=tracer_state, velocity=velocity, land_mask=land_mask, in_weight=in_weight, bias_one=bias_one, hid_weight=hid_weight, bias_two=bias_two, out_coef=out_coef, obs_cell=obs_cell, obs_count=obs_count, obs_value=obs_value, obs_var=obs_var, obs_noise=obs_noise)


def transport(concentration, velocity, sea_mask):
    east_open = sea_mask * jnp.roll(sea_mask, -1, axis=1)
    north_open = sea_mask * jnp.concatenate([sea_mask[1:], jnp.zeros_like(sea_mask[:1])], axis=0)
    east_speed = velocity[0] * east_open
    north_speed = velocity[1] * north_open
    for _ in range(ADV_STEPS):
        east_value = jnp.roll(concentration, -1, axis=-1)
        east_flux = jnp.maximum(east_speed, 0.0) * concentration + jnp.minimum(east_speed, 0.0) * east_value
        north_value = jnp.concatenate([concentration[..., 1:, :], jnp.zeros_like(concentration[..., :1, :])], axis=-2)
        north_flux = jnp.maximum(north_speed, 0.0) * concentration + jnp.minimum(north_speed, 0.0) * north_value
        west_flux = jnp.roll(east_flux, 1, axis=-1)
        south_flux = jnp.concatenate([jnp.zeros_like(north_flux[..., :1, :]), north_flux[..., :-1, :]], axis=-2)
        concentration = concentration - (east_flux - west_flux) - (north_flux - south_flux)
    return concentration

def reaction(fields, in_weight, bias_one, hid_weight, bias_two, member_coef, sea_cells):
    contract = (((0,), (0,)), ((), ()))
    hidden_one = lax.dot_general(in_weight.astype(jnp.float32), fields.astype(jnp.float32), contract, preferred_element_type=jnp.float32)
    hidden_one = jax.nn.silu(hidden_one + bias_one[:, None]).astype(jnp.bfloat16)
    hidden_two = lax.dot_general(hid_weight.astype(jnp.float32), hidden_one.astype(jnp.float32), contract, preferred_element_type=jnp.float32)
    hidden_two = jax.nn.silu(hidden_two + bias_two[:, None]).astype(jnp.bfloat16)
    tendency = jnp.dot(member_coef.astype(jnp.float32), hidden_two.astype(jnp.float32), preferred_element_type=jnp.float32) * hid_weight.shape[0] ** (-0.5)
    return ((fields.astype(jnp.float32) + tendency) * sea_cells).astype(jnp.bfloat16)

def solve_system(system, right_side):
    factor = jnp.linalg.cholesky(system)
    middle = lax.linalg.triangular_solve(factor, right_side, left_side=True, lower=True)
    return lax.linalg.triangular_solve(factor, middle, left_side=True, lower=True, transpose_a=True)

def reference(tracer_state, velocity, land_mask, in_weight, bias_one, hid_weight, bias_two, out_coef, obs_cell, obs_count, obs_value, obs_var, obs_noise):
    sea_mask = land_mask.astype(jnp.float32)
    fields_all = tracer_state.reshape(MEMBERS, NTR, LEV, LATS, LON)
    coef_half = out_coef.astype(jnp.bfloat16)
    sea_cells = jnp.broadcast_to(sea_mask[None], (LEV, LATS, LON)).reshape(-1)
    cell_index = jnp.broadcast_to(obs_cell[:, None, :], (BLOCKS, OBS_TR, OBS_CAP))

    def one_member(inputs):
        member_state, member_coef = inputs
        advected = transport(member_state.astype(jnp.float32) * sea_mask, velocity, sea_mask).astype(jnp.bfloat16)
        reacted = reaction(advected.reshape(NTR, -1), in_weight, bias_one, hid_weight, bias_two, member_coef, sea_cells)
        reacted = reacted.reshape(NTR, LEV, LATS, LON)
        observed = reacted[:OBS_TR].reshape(OBS_TR, LEV, BLOCKS, COL_DEV)
        observed = jnp.transpose(observed, (2, 0, 1, 3)).reshape(BLOCKS, OBS_TR, LEV * COL_DEV)
        picked = jnp.take_along_axis(observed, cell_index, axis=2)
        return (reacted, picked)
    new_fields, predicted = lax.map(one_member, (fields_all, coef_half))
    slot_ids = jnp.arange(OBS_CAP, dtype=jnp.int32)
    valid_slots = (slot_ids[None, :] < obs_count[:, None]).astype(jnp.float32)
    weight = valid_slots[:, None, :] / obs_var
    guessed = predicted.astype(jnp.float32).reshape(MEMBERS, -1)
    anomaly = guessed - jnp.mean(guessed, axis=0)
    misfit = (obs_value[None] + obs_noise).reshape(MEMBERS, -1) - guessed
    weighted = anomaly * weight.reshape(1, -1)
    highest = lax.Precision.HIGHEST
    gram = jnp.dot(weighted.astype(jnp.float32), anomaly.T.astype(jnp.float32), precision=highest, preferred_element_type=jnp.float32)
    cross = jnp.dot(weighted.astype(jnp.float32), misfit.T.astype(jnp.float32), precision=highest, preferred_element_type=jnp.float32)
    system = (MEMBERS - 1) * jnp.eye(MEMBERS, dtype=jnp.float32) + gram
    mixing = solve_system(system, cross)
    flat_coef = out_coef.reshape(MEMBERS, -1)
    new_coef = flat_coef + jnp.dot(mixing.T.astype(jnp.float32), flat_coef.astype(jnp.float32), precision=highest, preferred_element_type=jnp.float32)
    new_state = new_fields.reshape(MEMBERS * NTR, LEV, LATS, LON)
    return (new_state, new_coef.reshape(MEMBERS, NTR, HID))
```

```python
import functools

import jax
import jax.numpy as jnp
from jax import lax
from jax.experimental import pallas as pl
from jax.experimental.pallas import tpu as pltpu
from jax.sharding import PartitionSpec as P

OBS_TR = 6
ADV_STEPS = 2
OBS_CAP = 128
ROW_OCEAN = 1152
CHUNKS = 2
LANES = 128
FIELD_STEP = 4
WIDE = 384


def wrap_pad(buf, width):
    wide = buf.shape[-1]
    last = wide - LANES
    own = width - last
    tail = buf[..., last:]
    axis = tail.ndim - 1
    lane = lax.broadcasted_iota(jnp.int32, tail.shape, axis)
    east = pltpu.roll(buf[..., :LANES], own, axis)
    west = pltpu.roll(tail, LANES - own, axis)
    tail = jnp.where(lane < own, tail, jnp.where(lane < LANES - own, east, west))
    return jnp.concatenate([buf[..., :last], tail], axis=axis)


def transport_kernel(state_ref, velocity_ref, mask_ref, rank_ref, out_ref, coef, row, small, moved):
    fields, levels, lats, width = state_ref.shape
    wide = small.shape[-1]
    step_id = pl.program_id(0)

    @pl.when(step_id == 0)
    def _():
        small[:, :width] = mask_ref[...].astype(jnp.float32)
        sea = wrap_pad(small[...], width)
        row_ids = lax.broadcasted_iota(jnp.int32, sea.shape, 0)
        east_open = sea * pltpu.roll(sea, wide - 1, 1)
        north_open = jnp.where(row_ids < lats - 1, sea * pltpu.roll(sea, lats - 1, 0), 0.0)
        for level in range(levels):
            small[:, :width] = velocity_ref[0, level]
            east = wrap_pad(small[...], width) * east_open
            small[:, :width] = velocity_ref[1, level]
            north = wrap_pad(small[...], width) * north_open
            from_west = pltpu.roll(jnp.maximum(east, 0.0), 1, 1)
            from_south = pltpu.roll(jnp.maximum(north, 0.0), 1, 0)
            back_west = pltpu.roll(jnp.minimum(east, 0.0), 1, 1)
            back_south = pltpu.roll(jnp.minimum(north, 0.0), 1, 0)
            keep = 1.0 - (jnp.maximum(east, 0.0) - back_west)
            keep = keep - (jnp.maximum(north, 0.0) - back_south)
            coef[level, 0] = keep
            coef[level, 1] = -jnp.minimum(east, 0.0)
            coef[level, 2] = from_west
            coef[level, 3] = -jnp.minimum(north, 0.0)
            coef[level, 4] = from_south
            coef[level, 5] = sea

        for level in range(levels):

            def body(index, carry):
                first = index * FIELD_STEP
                row[..., :width] = state_ref[pl.ds(first, FIELD_STEP), level].astype(jnp.float32)
                value = wrap_pad(row[...], width) * coef[level, 5]
                for _ in range(ADV_STEPS):
                    value = (
                        coef[level, 0] * value
                        + coef[level, 1] * pltpu.roll(value, wide - 1, 2)
                        + coef[level, 2] * pltpu.roll(value, 1, 2)
                        + coef[level, 3] * pltpu.roll(value, lats - 1, 1)
                        + coef[level, 4] * pltpu.roll(value, 1, 1)
                    )
                start = pl.multiple_of((level * fields + first) * lats, FIELD_STEP * lats)
                value = value.reshape(FIELD_STEP * lats, wide)
                for tile in range(wide // LANES):
                    lanes = value[:, tile * LANES : (tile + 1) * LANES]
                    moved[tile, pl.ds(start, FIELD_STEP * lats)] = lanes
                return carry

            lax.fori_loop(0, fields // FIELD_STEP, body, 0)

    picked = pl.ds(step_id, levels * fields, stride=lats)
    source = [moved[tile, picked].astype(jnp.bfloat16) for tile in range(wide // LANES)]
    source = jnp.concatenate(source, axis=1)
    rank = rank_ref[0]
    for start in range(0, ROW_OCEAN, WIDE):
        slots = lax.broadcasted_iota(jnp.int32, (WIDE, wide), 0) + start
        pick = jnp.where(slots == rank, 1.0, 0.0).astype(jnp.bfloat16)
        packed = lax.dot_general(
            source, pick, (((1,), (1,)), ((), ())), preferred_element_type=jnp.float32
        )
        out_ref[0, :, :, :, start : start + WIDE] = packed.reshape(
            out_ref.shape[1:4] + (WIDE,)
        ).astype(jnp.bfloat16)


def transport_packed(tracer_state, velocity, land_mask, rank, tracers, chunk):
    fields, levels, lats, width = tracer_state.shape
    wide = rank.shape[-1]
    part = levels // CHUNKS
    return pl.pallas_call(
        transport_kernel,
        grid=(lats,),
        in_specs=[
            pl.BlockSpec((fields, part, lats, width), lambda k: (0, chunk, 0, 0)),
            pl.BlockSpec((2, part, lats, width), lambda k: (0, chunk, 0, 0)),
            pl.BlockSpec((lats, width), lambda k: (0, 0)),
            pl.BlockSpec((1, 1, wide), lambda k: (k, 0, 0)),
        ],
        out_specs=pl.BlockSpec(
            (1, part, fields // tracers, tracers, ROW_OCEAN), lambda k: (k, 0, 0, 0, 0)
        ),
        out_shape=jax.ShapeDtypeStruct(
            (lats, part, fields // tracers, tracers, ROW_OCEAN), jnp.bfloat16
        ),
        scratch_shapes=[
            pltpu.VMEM((part, 6, lats, wide), jnp.float32),
            pltpu.VMEM((FIELD_STEP, lats, wide), jnp.float32),
            pltpu.VMEM((lats, wide), jnp.float32),
            pltpu.VMEM((wide // LANES, part * fields * lats, LANES), jnp.float32),
        ],
        compiler_params=pltpu.CompilerParams(vmem_limit_bytes=48 * 1024 * 1024),
        cost_estimate=pl.CostEstimate(
            flops=2 * part * fields * lats * wide * ROW_OCEAN,
            bytes_accessed=4 * part * fields * lats * width,
            transcendentals=0,
        ),
        name="transport",
    )(tracer_state, velocity, land_mask, rank[:, None])


def half_silu(half):
    return (half + half * jnp.tanh(half)).astype(jnp.bfloat16)


def reaction_kernel(
    first_level,
    packed_ref,
    in_ref,
    bias_one_ref,
    hid_ref,
    bias_two_ref,
    coef_ref,
    rank_ref,
    cell_ref,
    *rest,
):
    out_ref, seen_ref, spread, fresh = rest[-4:]
    sources, _, per_source, tracers, slots = packed_ref.shape
    width = out_ref.shape[1]
    members = coef_ref.shape[0]
    hidden = hid_ref.shape[0]

    @pl.when(pl.program_id(0) == 0)
    def _():
        for start in range(0, slots, LANES):
            ids = lax.broadcasted_iota(jnp.int32, (width, LANES), 1) + start
            same = jnp.where(ids == rank_ref[...], 1.0, 0.0)
            spread[:, start : start + LANES] = same.astype(jnp.bfloat16)

    def body(index, carry):
        both = []
        for half in range(2):
            member = 2 * index + half
            source = lax.div(member, per_source)
            inner = lax.rem(member, per_source)
            parts = []
            for start in range(0, slots, WIDE):
                fields = packed_ref[source, 0, inner, :, start : start + WIDE]
                one = jnp.dot(in_ref[...], fields, preferred_element_type=jnp.float32)
                one = half_silu(one + bias_one_ref[...])
                two = jnp.dot(hid_ref[...], one, preferred_element_type=jnp.float32)
                two = half_silu(two + bias_two_ref[...])
                change = jnp.dot(coef_ref[member], two, preferred_element_type=jnp.float32)
                parts.append(fields.astype(jnp.float32) + change * hidden ** (-0.5))
            both.append(jnp.concatenate(parts, axis=1))
        pair = jnp.concatenate(both, axis=0).astype(jnp.bfloat16)
        fresh[pl.ds(pl.multiple_of(index * 2 * tracers, 16), 2 * tracers)] = pair
        return carry

    lax.fori_loop(0, members // 2, body, 0)
    cells = lax.dot_general(
        spread[...], fresh[...], (((1,), (1,)), ((), ())), preferred_element_type=jnp.float32
    ).astype(jnp.bfloat16)
    out_ref[0] = cells
    level = first_level + pl.program_id(0)
    ids = lax.broadcasted_iota(jnp.int32, (OBS_CAP, width), 1) + level * width
    pick = jnp.where(ids == cell_ref[...], 1.0, 0.0).astype(jnp.bfloat16)
    seen = jnp.dot(pick, cells, preferred_element_type=jnp.float32)

    @pl.when(pl.program_id(0) == 0)
    def _():
        seen_ref[...] = seen

    @pl.when(pl.program_id(0) > 0)
    def _():
        seen_ref[...] += seen


def reaction(
    packed, in_t, bias_one, hid_t, bias_two, coef_half, rank_own, obs_cell, levels, first, earlier
):
    sources, part, per_source, tracers, slots = packed.shape
    members, _, hidden = coef_half.shape
    width = rank_own.shape[0]
    rows = members * tracers
    whole = lambda *dims: pl.BlockSpec(dims, lambda level: (0,) * len(dims))
    return pl.pallas_call(
        functools.partial(reaction_kernel, first),
        grid=(part,),
        in_specs=[
            pl.BlockSpec(
                (sources, 1, per_source, tracers, slots), lambda level: (0, level, 0, 0, 0)
            ),
            whole(hidden, tracers),
            whole(hidden, 1),
            whole(hidden, hidden),
            whole(hidden, 1),
            whole(members, tracers, hidden),
            whole(*rank_own.shape),
            whole(OBS_CAP, 1),
        ]
        + [pl.BlockSpec(memory_space=pl.ANY)] * len(earlier),
        out_specs=[
            pl.BlockSpec((1, width, rows), lambda level: (first + level, 0, 0)),
            whole(OBS_CAP, rows),
        ],
        out_shape=[
            jax.ShapeDtypeStruct((levels, width, rows), jnp.bfloat16),
            jax.ShapeDtypeStruct((OBS_CAP, rows), jnp.float32),
        ],
        input_output_aliases={8: 0} if earlier else {},
        scratch_shapes=[
            pltpu.VMEM((width, slots), jnp.bfloat16),
            pltpu.VMEM((rows, slots), jnp.bfloat16),
        ],
        compiler_params=pltpu.CompilerParams(vmem_limit_bytes=48 * 1024 * 1024),
        cost_estimate=pl.CostEstimate(
            flops=2 * part * rows * slots * (width + 2 * hidden + hidden * hidden // tracers),
            bytes_accessed=2 * part * rows * (slots + width),
            transcendentals=2 * part * members * slots * hidden,
        ),
        name="reaction",
    )(packed, in_t, bias_one, hid_t, bias_two, coef_half, rank_own, obs_cell, *earlier)


def solve_system(system, right_side):
    factor = jnp.linalg.cholesky(system)
    middle = lax.linalg.triangular_solve(factor, right_side, left_side=True, lower=True)
    return lax.linalg.triangular_solve(factor, middle, left_side=True, lower=True, transpose_a=True)


def shards(
    tracer_state,
    velocity,
    land_mask,
    in_weight,
    bias_one,
    hid_weight,
    bias_two,
    out_coef,
    obs_cell,
    obs_count,
    obs_value,
    obs_var,
    obs_noise,
):
    own_block = lax.axis_index("trc")
    group_index = lax.axis_index("ens")
    field_rows, levels, lat_rows, lon_count = tracer_state.shape
    members_here = out_coef.shape[0]
    tracers = in_weight.shape[0]
    group_rows = members_here * tracers
    highest = lax.Precision.HIGHEST
    wide = -(-lon_count // LANES) * LANES
    below = jnp.arange(lon_count)[:, None] < jnp.arange(lon_count)[None, :]
    before = jnp.dot(
        land_mask.astype(jnp.bfloat16), below.astype(jnp.bfloat16), preferred_element_type=jnp.float32
    )
    rank = jnp.where(land_mask > 0, before.astype(jnp.int32), -1)
    rank = jnp.pad(rank, ((0, 0), (0, wide - lon_count)), constant_values=-1)
    rank_own = lax.dynamic_slice_in_dim(rank, own_block, 1, 0)[:, :lon_count].T
    coef_half = out_coef.astype(jnp.bfloat16)
    in_t = in_weight.T * jnp.bfloat16(0.5)
    hid_t = hid_weight.T * jnp.bfloat16(0.5)
    half_one = bias_one[:, None] * 0.5
    half_two = bias_two[:, None] * 0.5
    part = levels // CHUNKS
    received = []
    for chunk in range(CHUNKS):
        packed = transport_packed(tracer_state, velocity, land_mask, rank, tracers, chunk)
        received.append(lax.all_to_all(packed, "trc", split_axis=0, concat_axis=0, tiled=True))
    earlier = []
    predicted = 0.0
    for chunk in range(CHUNKS):
        cells, seen = reaction(
            received[chunk],
            in_t,
            half_one,
            hid_t,
            half_two,
            coef_half,
            rank_own,
            obs_cell.T,
            levels,
            chunk * part,
            earlier,
        )
        earlier = [cells]
        predicted = predicted + seen
    new_cols = jnp.transpose(earlier[0], (2, 0, 1))[:, :, None]
    predicted_own = predicted.T.reshape(members_here, tracers, OBS_CAP)[:, :OBS_TR]
    predicted_own = predicted_own.astype(jnp.bfloat16)
    predicted_all = lax.all_gather(predicted_own, "ens", axis=0, tiled=True)
    member_total = predicted_all.shape[0]
    slot_ids = jnp.arange(OBS_CAP, dtype=jnp.int32)
    valid_slots = (slot_ids < obs_count[0]).astype(jnp.float32)
    weight = valid_slots[None, :] / obs_var[0]
    guessed = predicted_all.astype(jnp.float32).reshape(member_total, -1)
    anomaly = guessed - jnp.mean(guessed, axis=0)
    misfit = (obs_value[None] + obs_noise).reshape(member_total, -1) - guessed
    weighted = anomaly * weight.reshape(1, -1)
    terms = jnp.dot(
        weighted,
        jnp.concatenate([anomaly, misfit], axis=0).T,
        precision=highest,
        preferred_element_type=jnp.float32,
    )
    terms = jnp.sum(lax.all_gather(terms, "trc", axis=0), axis=0)
    gram, cross = terms[:, :member_total], terms[:, member_total:]
    system = (member_total - 1) * jnp.eye(member_total, dtype=jnp.float32) + gram
    mixing = solve_system(system, cross)
    flat_coef = out_coef.reshape(members_here, -1)
    first_member = group_index * members_here
    mixing_rows = lax.dynamic_slice_in_dim(mixing, first_member, members_here, 0)
    summed = lax.psum_scatter(
        jnp.dot(mixing_rows.T, flat_coef, precision=highest, preferred_element_type=jnp.float32),
        "ens",
        scatter_dimension=0,
        tiled=True,
    )
    new_coef = flat_coef + summed
    return (new_cols, new_coef.reshape(members_here, tracers, -1))


def solution(mesh):
    in_specs = (
        P(("ens", "trc"), None, None, None),
        P(),
        P(),
        P(),
        P(),
        P(),
        P(),
        P("ens", None, None),
        P("trc", None),
        P("trc"),
        P("trc", None, None),
        P("trc", None, None),
        P(None, "trc", None, None),
    )
    out_specs = (P("ens", None, "trc", None), P("ens", None, None))
    return jax.shard_map(shards, mesh=mesh, in_specs=in_specs, out_specs=out_specs, check_vma=False)
```

```python
import functools

import jax
import jax.numpy as jnp
from jax import lax
from jax.experimental import pallas as pl
from jax.experimental.pallas import tpu as pltpu
from jax.sharding import PartitionSpec as P

OBS_TR = 6
ADV_STEPS = 2
OBS_CAP = 128
ROW_OCEAN = 1152
CHUNKS = 2
LANES = 128
FIELD_STEP = 4
WIDE = 384


def wrap_pad(buf, width):
    wide = buf.shape[-1]
    last = wide - LANES
    own = width - last
    tail = buf[..., last:]
    axis = tail.ndim - 1
    lane = lax.broadcasted_iota(jnp.int32, tail.shape, axis)
    east = pltpu.roll(buf[..., :LANES], own, axis)
    west = pltpu.roll(tail, LANES - own, axis)
    tail = jnp.where(lane < own, tail, jnp.where(lane < LANES - own, east, west))
    return jnp.concatenate([buf[..., :last], tail], axis=axis)


def transport_kernel(state_ref, velocity_ref, mask_ref, rank_ref, out_ref, coef, row, small, moved):
    fields, levels, lats, width = state_ref.shape
    wide = small.shape[-1]
    step_id = pl.program_id(0)

    @pl.when(step_id == 0)
    def _():
        small[:, :width] = mask_ref[...].astype(jnp.float32)
        sea = wrap_pad(small[...], width)
        row_ids = lax.broadcasted_iota(jnp.int32, sea.shape, 0)
        east_open = sea * pltpu.roll(sea, wide - 1, 1)
        north_open = jnp.where(row_ids < lats - 1, sea * pltpu.roll(sea, lats - 1, 0), 0.0)
        for level in range(levels):
            small[:, :width] = velocity_ref[0, level]
            east = wrap_pad(small[...], width) * east_open
            small[:, :width] = velocity_ref[1, level]
            north = wrap_pad(small[...], width) * north_open
            from_west = pltpu.roll(jnp.maximum(east, 0.0), 1, 1)
            from_south = pltpu.roll(jnp.maximum(north, 0.0), 1, 0)
            back_west = pltpu.roll(jnp.minimum(east, 0.0), 1, 1)
            back_south = pltpu.roll(jnp.minimum(north, 0.0), 1, 0)
            keep = 1.0 - (jnp.maximum(east, 0.0) - back_west)
            keep = keep - (jnp.maximum(north, 0.0) - back_south)
            coef[level, 0] = keep
            coef[level, 1] = -jnp.minimum(east, 0.0)
            coef[level, 2] = from_west
            coef[level, 3] = -jnp.minimum(north, 0.0)
            coef[level, 4] = from_south
            coef[level, 5] = sea

        for level in range(levels):

            def body(index, carry):
                first = index * FIELD_STEP
                row[..., :width] = state_ref[pl.ds(first, FIELD_STEP), level].astype(jnp.float32)
                value = wrap_pad(row[...], width) * coef[level, 5]
                for _ in range(ADV_STEPS):
                    value = (
                        coef[level, 0] * value
                        + coef[level, 1] * pltpu.roll(value, wide - 1, 2)
                        + coef[level, 2] * pltpu.roll(value, 1, 2)
                        + coef[level, 3] * pltpu.roll(value, lats - 1, 1)
                        + coef[level, 4] * pltpu.roll(value, 1, 1)
                    )
                start = pl.multiple_of((level * fields + first) * lats, FIELD_STEP * lats)
                value = value.reshape(FIELD_STEP * lats, wide)
                for tile in range(wide // LANES):
                    lanes = value[:, tile * LANES : (tile + 1) * LANES]
                    moved[tile, pl.ds(start, FIELD_STEP * lats)] = lanes
                return carry

            lax.fori_loop(0, fields // FIELD_STEP, body, 0)

    picked = pl.ds(step_id, levels * fields, stride=lats)
    source = [moved[tile, picked].astype(jnp.bfloat16) for tile in range(wide // LANES)]
    source = jnp.concatenate(source, axis=1)
    rank = rank_ref[0]
    for start in range(0, ROW_OCEAN, WIDE):
        slots = lax.broadcasted_iota(jnp.int32, (WIDE, wide), 0) + start
        pick = jnp.where(slots == rank, 1.0, 0.0).astype(jnp.bfloat16)
        packed = lax.dot_general(
            source, pick, (((1,), (1,)), ((), ())), preferred_element_type=jnp.float32
        )
        out_ref[0, :, :, :, start : start + WIDE] = packed.reshape(
            out_ref.shape[1:4] + (WIDE,)
        ).astype(jnp.bfloat16)


def transport_packed(tracer_state, velocity, land_mask, rank, tracers, chunk):
    fields, levels, lats, width = tracer_state.shape
    wide = rank.shape[-1]
    part = levels // CHUNKS
    return pl.pallas_call(
        transport_kernel,
        grid=(lats,),
        in_specs=[
            pl.BlockSpec((fields, part, lats, width), lambda k: (0, chunk, 0, 0)),
            pl.BlockSpec((2, part, lats, width), lambda k: (0, chunk, 0, 0)),
            pl.BlockSpec((lats, width), lambda k: (0, 0)),
            pl.BlockSpec((1, 1, wide), lambda k: (k, 0, 0)),
        ],
        out_specs=pl.BlockSpec(
            (1, part, fields // tracers, tracers, ROW_OCEAN), lambda k: (k, 0, 0, 0, 0)
        ),
        out_shape=jax.ShapeDtypeStruct(
            (lats, part, fields // tracers, tracers, ROW_OCEAN), jnp.bfloat16
        ),
        scratch_shapes=[
            pltpu.VMEM((part, 6, lats, wide), jnp.float32),
            pltpu.VMEM((FIELD_STEP, lats, wide), jnp.float32),
            pltpu.VMEM((lats, wide), jnp.float32),
            pltpu.VMEM((wide // LANES, part * fields * lats, LANES), jnp.float32),
        ],
        compiler_params=pltpu.CompilerParams(vmem_limit_bytes=48 * 1024 * 1024),
        cost_estimate=pl.CostEstimate(
            flops=2 * part * fields * lats * wide * ROW_OCEAN,
            bytes_accessed=4 * part * fields * lats * width,
            transcendentals=0,
        ),
        name="transport",
    )(tracer_state, velocity, land_mask, rank[:, None])


def half_silu(half):
    half = half.astype(jnp.bfloat16)
    return half * (jnp.tanh(half) + jnp.bfloat16(1.0))


def reaction_kernel(
    first_level,
    packed_ref,
    in_ref,
    bias_one_ref,
    hid_ref,
    bias_two_ref,
    coef_ref,
    rank_ref,
    cell_ref,
    *rest,
):
    out_ref, seen_ref, spread, fresh = rest[-4:]
    sources, _, per_source, tracers, slots = packed_ref.shape
    width = out_ref.shape[1]
    members = coef_ref.shape[0]
    hidden = hid_ref.shape[0]

    @pl.when(pl.program_id(0) == 0)
    def _():
        for start in range(0, slots, LANES):
            ids = lax.broadcasted_iota(jnp.int32, (width, LANES), 1) + start
            same = jnp.where(ids == rank_ref[...], 1.0, 0.0)
            spread[:, start : start + LANES] = same.astype(jnp.bfloat16)

    def body(index, carry):
        both = []
        for half in range(2):
            member = 2 * index + half
            source = lax.div(member, per_source)
            inner = lax.rem(member, per_source)
            parts = []
            for start in range(0, slots, WIDE):
                fields = packed_ref[source, 0, inner, :, start : start + WIDE]
                one = jnp.dot(in_ref[...], fields, preferred_element_type=jnp.float32)
                one = half_silu(one + bias_one_ref[...])
                two = jnp.dot(hid_ref[...], one, preferred_element_type=jnp.float32)
                two = half_silu(two + bias_two_ref[...])
                change = jnp.dot(coef_ref[member], two, preferred_element_type=jnp.float32)
                parts.append(fields.astype(jnp.float32) + change * hidden ** (-0.5))
            both.append(jnp.concatenate(parts, axis=1))
        pair = jnp.concatenate(both, axis=0).astype(jnp.bfloat16)
        fresh[pl.ds(pl.multiple_of(index * 2 * tracers, 16), 2 * tracers)] = pair
        return carry

    lax.fori_loop(0, members // 2, body, 0)
    cells = lax.dot_general(
        spread[...], fresh[...], (((1,), (1,)), ((), ())), preferred_element_type=jnp.float32
    ).astype(jnp.bfloat16)
    out_ref[0] = cells
    level = first_level + pl.program_id(0)
    ids = lax.broadcasted_iota(jnp.int32, (OBS_CAP, width), 1) + level * width
    pick = jnp.where(ids == cell_ref[...], 1.0, 0.0).astype(jnp.bfloat16)
    seen = jnp.dot(pick, cells, preferred_element_type=jnp.float32)

    @pl.when(pl.program_id(0) == 0)
    def _():
        seen_ref[...] = seen

    @pl.when(pl.program_id(0) > 0)
    def _():
        seen_ref[...] += seen


def reaction(
    packed, in_t, bias_one, hid_t, bias_two, coef_half, rank_own, obs_cell, levels, first, earlier
):
    sources, part, per_source, tracers, slots = packed.shape
    members, _, hidden = coef_half.shape
    width = rank_own.shape[0]
    rows = members * tracers
    whole = lambda *dims: pl.BlockSpec(dims, lambda level: (0,) * len(dims))
    return pl.pallas_call(
        functools.partial(reaction_kernel, first),
        grid=(part,),
        in_specs=[
            pl.BlockSpec(
                (sources, 1, per_source, tracers, slots), lambda level: (0, level, 0, 0, 0)
            ),
            whole(hidden, tracers),
            whole(hidden, 1),
            whole(hidden, hidden),
            whole(hidden, 1),
            whole(members, tracers, hidden),
            whole(*rank_own.shape),
            whole(OBS_CAP, 1),
        ]
        + [pl.BlockSpec(memory_space=pl.ANY)] * len(earlier),
        out_specs=[
            pl.BlockSpec((1, width, rows), lambda level: (first + level, 0, 0)),
            whole(OBS_CAP, rows),
        ],
        out_shape=[
            jax.ShapeDtypeStruct((levels, width, rows), jnp.bfloat16),
            jax.ShapeDtypeStruct((OBS_CAP, rows), jnp.float32),
        ],
        input_output_aliases={8: 0} if earlier else {},
        scratch_shapes=[
            pltpu.VMEM((width, slots), jnp.bfloat16),
            pltpu.VMEM((rows, slots), jnp.bfloat16),
        ],
        compiler_params=pltpu.CompilerParams(vmem_limit_bytes=48 * 1024 * 1024),
        cost_estimate=pl.CostEstimate(
            flops=2 * part * rows * slots * (width + 2 * hidden + hidden * hidden // tracers),
            bytes_accessed=2 * part * rows * (slots + width),
            transcendentals=2 * part * members * slots * hidden,
        ),
        name="reaction",
    )(packed, in_t, bias_one, hid_t, bias_two, coef_half, rank_own, obs_cell, *earlier)


def sum_kernel(count, term_ref, out_ref, slots, send_sem, recv_sem):
    own = lax.axis_index("trc")
    peers = [lax.rem(own + step, count) for step in range(1, count)]
    barrier = pltpu.get_barrier_semaphore()
    for peer in peers:
        pl.semaphore_signal(
            barrier, inc=1, device_id={"trc": peer}, device_id_type=pl.DeviceIdType.MESH
        )
    pl.semaphore_wait(barrier, count - 1)
    copies = []
    for step, peer in enumerate(peers):
        copy = pltpu.make_async_remote_copy(
            src_ref=term_ref,
            dst_ref=slots.at[own],
            send_sem=send_sem.at[step],
            recv_sem=recv_sem.at[step],
            device_id={"trc": peer},
            device_id_type=pl.DeviceIdType.MESH,
        )
        copy.start()
        copies.append(copy)
    slots[own] = term_ref[...]
    for copy in copies:
        copy.wait()
    total = slots[0]
    for source in range(1, count):
        total = total + slots[source]
    out_ref[...] = total


def sum_over_blocks(terms):
    count = lax.axis_size("trc")
    return pl.pallas_call(
        functools.partial(sum_kernel, count),
        in_specs=[pl.BlockSpec(memory_space=pltpu.VMEM)],
        out_specs=pl.BlockSpec(memory_space=pltpu.VMEM),
        out_shape=jax.ShapeDtypeStruct(terms.shape, terms.dtype),
        scratch_shapes=[
            pltpu.VMEM((count,) + terms.shape, terms.dtype),
            pltpu.SemaphoreType.DMA((count - 1,)),
            pltpu.SemaphoreType.DMA((count - 1,)),
        ],
        compiler_params=pltpu.CompilerParams(
            collective_id=0, has_side_effects=True, vmem_limit_bytes=16 * 1024 * 1024
        ),
        name="block_sum",
    )(terms)


def solve_system(system, right_side):
    factor = jnp.linalg.cholesky(system)
    middle = lax.linalg.triangular_solve(factor, right_side, left_side=True, lower=True)
    return lax.linalg.triangular_solve(factor, middle, left_side=True, lower=True, transpose_a=True)


def shards(
    tracer_state,
    velocity,
    land_mask,
    in_weight,
    bias_one,
    hid_weight,
    bias_two,
    out_coef,
    obs_cell,
    obs_count,
    obs_value,
    obs_var,
    obs_noise,
):
    own_block = lax.axis_index("trc")
    group_index = lax.axis_index("ens")
    field_rows, levels, lat_rows, lon_count = tracer_state.shape
    members_here = out_coef.shape[0]
    tracers = in_weight.shape[0]
    group_rows = members_here * tracers
    highest = lax.Precision.HIGHEST
    wide = -(-lon_count // LANES) * LANES
    below = jnp.arange(lon_count)[:, None] < jnp.arange(lon_count)[None, :]
    before = jnp.dot(
        land_mask.astype(jnp.bfloat16), below.astype(jnp.bfloat16), preferred_element_type=jnp.float32
    )
    rank = jnp.where(land_mask > 0, before.astype(jnp.int32), -1)
    rank = jnp.pad(rank, ((0, 0), (0, wide - lon_count)), constant_values=-1)
    rank_own = lax.dynamic_slice_in_dim(rank, own_block, 1, 0)[:, :lon_count].T
    coef_half = out_coef.astype(jnp.bfloat16)
    in_t = in_weight.T * jnp.bfloat16(0.5)
    hid_t = hid_weight.T * jnp.bfloat16(0.5)
    half_one = bias_one[:, None] * 0.5
    half_two = bias_two[:, None] * 0.5
    flat_coef = out_coef.reshape(members_here, -1)
    coef_all = lax.all_gather(flat_coef, "ens", axis=0, tiled=True)
    obs_own = (obs_value[None] + obs_noise).reshape(obs_noise.shape[0], -1)
    cell_column = obs_cell.T
    part = levels // CHUNKS
    received = []
    for chunk in range(CHUNKS):
        if chunk == 1:
            ready = (rank, rank_own, coef_half, in_t, hid_t, half_one, half_two, cell_column, obs_own)
            ready = lax.optimization_barrier(ready)
            rank, rank_own, coef_half, in_t, hid_t, half_one, half_two, cell_column, obs_own = ready
        packed = transport_packed(tracer_state, velocity, land_mask, rank, tracers, chunk)
        received.append(lax.all_to_all(packed, "trc", split_axis=0, concat_axis=0, tiled=True))
    earlier = []
    predicted = 0.0
    for chunk in range(CHUNKS):
        cells, seen = reaction(
            received[chunk],
            in_t,
            half_one,
            hid_t,
            half_two,
            coef_half,
            rank_own,
            cell_column,
            levels,
            chunk * part,
            earlier,
        )
        earlier = [cells]
        predicted = predicted + seen
    new_cols = jnp.transpose(earlier[0], (2, 0, 1))[:, :, None]
    predicted_own = predicted.T.reshape(members_here, tracers, OBS_CAP)[:, :OBS_TR]
    predicted_own = predicted_own.astype(jnp.bfloat16)
    predicted_all = lax.all_gather(predicted_own, "ens", axis=0, tiled=True)
    member_total = predicted_all.shape[0]
    slot_ids = jnp.arange(OBS_CAP, dtype=jnp.int32)
    valid_slots = (slot_ids < obs_count[0]).astype(jnp.float32)
    weight = valid_slots[None, :] / obs_var[0]
    guessed = predicted_all.astype(jnp.float32).reshape(member_total, -1)
    anomaly = guessed - jnp.mean(guessed, axis=0)
    misfit = obs_own - guessed
    weighted = anomaly * weight.reshape(1, -1)
    terms = jnp.dot(
        weighted,
        jnp.concatenate([anomaly, misfit], axis=0).T,
        precision=highest,
        preferred_element_type=jnp.float32,
    )
    terms = sum_over_blocks(terms)
    gram, cross = terms[:, :member_total], terms[:, member_total:]
    system = (member_total - 1) * jnp.eye(member_total, dtype=jnp.float32) + gram
    mixing = solve_system(system, cross)
    first_member = group_index * members_here
    mixing_own = lax.dynamic_slice_in_dim(mixing, first_member, members_here, 1)
    summed = jnp.dot(
        mixing_own.T, coef_all, precision=highest, preferred_element_type=jnp.float32
    )
    new_coef = flat_coef + summed
    return (new_cols, new_coef.reshape(members_here, tracers, -1))


def solution(mesh):
    in_specs = (
        P(("ens", "trc"), None, None, None),
        P(),
        P(),
        P(),
        P(),
        P(),
        P(),
        P("ens", None, None),
        P("trc", None),
        P("trc"),
        P("trc", None, None),
        P("trc", None, None),
        P(None, "trc", None, None),
    )
    out_specs = (P("ens", None, "trc", None), P("ens", None, None))
    return jax.shard_map(shards, mesh=mesh, in_specs=in_specs, out_specs=out_specs, check_vma=False)
```

```python
import functools

import jax
import jax.numpy as jnp
from jax import lax
from jax.experimental import pallas as pl
from jax.experimental.pallas import tpu as pltpu
from jax.sharding import PartitionSpec as P

OBS_TR = 6
ADV_STEPS = 2
OBS_CAP = 128
ROW_OCEAN = 1152
CHUNKS = 2
LANES = 128
FIELD_STEP = 4
WIDE = 384


def wrap_pad(buf, width):
    wide = buf.shape[-1]
    last = wide - LANES
    own = width - last
    tail = buf[..., last:]
    axis = tail.ndim - 1
    lane = lax.broadcasted_iota(jnp.int32, tail.shape, axis)
    east = pltpu.roll(buf[..., :LANES], own, axis)
    west = pltpu.roll(tail, LANES - own, axis)
    tail = jnp.where(lane < own, tail, jnp.where(lane < LANES - own, east, west))
    return jnp.concatenate([buf[..., :last], tail], axis=axis)


def transport_kernel(state_ref, velocity_ref, mask_ref, rank_ref, out_ref, coef, row, small, moved):
    fields, levels, lats, width = state_ref.shape
    wide = small.shape[-1]
    step_id = pl.program_id(0)

    @pl.when(step_id == 0)
    def _():
        small[:, :width] = mask_ref[...].astype(jnp.float32)
        sea = wrap_pad(small[...], width)
        row_ids = lax.broadcasted_iota(jnp.int32, sea.shape, 0)
        east_open = sea * pltpu.roll(sea, wide - 1, 1)
        north_open = jnp.where(row_ids < lats - 1, sea * pltpu.roll(sea, lats - 1, 0), 0.0)
        for level in range(levels):
            small[:, :width] = velocity_ref[0, level]
            east = wrap_pad(small[...], width) * east_open
            small[:, :width] = velocity_ref[1, level]
            north = wrap_pad(small[...], width) * north_open
            from_west = pltpu.roll(jnp.maximum(east, 0.0), 1, 1)
            from_south = pltpu.roll(jnp.maximum(north, 0.0), 1, 0)
            back_west = pltpu.roll(jnp.minimum(east, 0.0), 1, 1)
            back_south = pltpu.roll(jnp.minimum(north, 0.0), 1, 0)
            keep = 1.0 - (jnp.maximum(east, 0.0) - back_west)
            keep = keep - (jnp.maximum(north, 0.0) - back_south)
            coef[level, 0] = keep
            coef[level, 1] = -jnp.minimum(east, 0.0)
            coef[level, 2] = from_west
            coef[level, 3] = -jnp.minimum(north, 0.0)
            coef[level, 4] = from_south
            coef[level, 5] = sea

        for level in range(levels):

            def body(index, carry):
                first = index * FIELD_STEP
                row[..., :width] = state_ref[pl.ds(first, FIELD_STEP), level].astype(jnp.float32)
                value = wrap_pad(row[...], width) * coef[level, 5]
                for _ in range(ADV_STEPS):
                    value = (
                        coef[level, 0] * value
                        + coef[level, 1] * pltpu.roll(value, wide - 1, 2)
                        + coef[level, 2] * pltpu.roll(value, 1, 2)
                        + coef[level, 3] * pltpu.roll(value, lats - 1, 1)
                        + coef[level, 4] * pltpu.roll(value, 1, 1)
                    )
                start = pl.multiple_of((level * fields + first) * lats, FIELD_STEP * lats)
                value = value.reshape(FIELD_STEP * lats, wide)
                for tile in range(wide // LANES):
                    lanes = value[:, tile * LANES : (tile + 1) * LANES]
                    moved[tile, pl.ds(start, FIELD_STEP * lats)] = lanes
                return carry

            lax.fori_loop(0, fields // FIELD_STEP, body, 0)

    picked = pl.ds(step_id, levels * fields, stride=lats)
    source = [moved[tile, picked].astype(jnp.bfloat16) for tile in range(wide // LANES)]
    source = jnp.concatenate(source, axis=1)
    rank = rank_ref[0]
    for start in range(0, ROW_OCEAN, WIDE):
        slots = lax.broadcasted_iota(jnp.int32, (WIDE, wide), 0) + start
        pick = jnp.where(slots == rank, 1.0, 0.0).astype(jnp.bfloat16)
        packed = lax.dot_general(
            source, pick, (((1,), (1,)), ((), ())), preferred_element_type=jnp.float32
        )
        out_ref[0, :, :, :, start : start + WIDE] = packed.reshape(
            out_ref.shape[1:4] + (WIDE,)
        ).astype(jnp.bfloat16)


def transport_packed(tracer_state, velocity, land_mask, rank, tracers, chunk):
    fields, levels, lats, width = tracer_state.shape
    wide = rank.shape[-1]
    part = levels // CHUNKS
    return pl.pallas_call(
        transport_kernel,
        grid=(lats,),
        in_specs=[
            pl.BlockSpec((fields, part, lats, width), lambda k: (0, chunk, 0, 0)),
            pl.BlockSpec((2, part, lats, width), lambda k: (0, chunk, 0, 0)),
            pl.BlockSpec((lats, width), lambda k: (0, 0)),
            pl.BlockSpec((1, 1, wide), lambda k: (k, 0, 0)),
        ],
        out_specs=pl.BlockSpec(
            (1, part, fields // tracers, tracers, ROW_OCEAN), lambda k: (k, 0, 0, 0, 0)
        ),
        out_shape=jax.ShapeDtypeStruct(
            (lats, part, fields // tracers, tracers, ROW_OCEAN), jnp.bfloat16
        ),
        scratch_shapes=[
            pltpu.VMEM((part, 6, lats, wide), jnp.float32),
            pltpu.VMEM((FIELD_STEP, lats, wide), jnp.float32),
            pltpu.VMEM((lats, wide), jnp.float32),
            pltpu.VMEM((wide // LANES, part * fields * lats, LANES), jnp.float32),
        ],
        compiler_params=pltpu.CompilerParams(vmem_limit_bytes=48 * 1024 * 1024),
        cost_estimate=pl.CostEstimate(
            flops=2 * part * fields * lats * wide * ROW_OCEAN,
            bytes_accessed=4 * part * fields * lats * width,
            transcendentals=0,
        ),
        name="transport",
    )(tracer_state, velocity, land_mask, rank[:, None])


def half_silu(half):
    return (half + half * jnp.tanh(half)).astype(jnp.bfloat16)


def reaction_kernel(
    first_level,
    packed_ref,
    in_ref,
    bias_one_ref,
    hid_ref,
    bias_two_ref,
    coef_ref,
    rank_ref,
    cell_ref,
    *rest,
):
    out_ref, seen_ref, spread, fresh = rest[-4:]
    sources, _, per_source, tracers, slots = packed_ref.shape
    width = out_ref.shape[1]
    members = coef_ref.shape[0]
    hidden = hid_ref.shape[0]

    @pl.when(pl.program_id(0) == 0)
    def _():
        for start in range(0, slots, LANES):
            ids = lax.broadcasted_iota(jnp.int32, (width, LANES), 1) + start
            same = jnp.where(ids == rank_ref[...], 1.0, 0.0)
            spread[:, start : start + LANES] = same.astype(jnp.bfloat16)

    def body(index, carry):
        both = []
        for half in range(2):
            member = 2 * index + half
            source = lax.div(member, per_source)
            inner = lax.rem(member, per_source)
            fields = packed_ref[source, 0, inner]
            one = jnp.dot(in_ref[...], fields, preferred_element_type=jnp.float32)
            one = half_silu(one + bias_one_ref[...])
            two = jnp.dot(hid_ref[...], one, preferred_element_type=jnp.float32)
            two = half_silu(two + bias_two_ref[...])
            change = jnp.dot(coef_ref[member], two, preferred_element_type=jnp.float32)
            both.append(fields.astype(jnp.float32) + change * hidden ** (-0.5))
        pair = jnp.concatenate(both, axis=0).astype(jnp.bfloat16)
        fresh[pl.ds(pl.multiple_of(index * 2 * tracers, 16), 2 * tracers)] = pair
        return carry

    lax.fori_loop(0, members // 2, body, 0)
    cells = lax.dot_general(
        spread[...], fresh[...], (((1,), (1,)), ((), ())), preferred_element_type=jnp.float32
    ).astype(jnp.bfloat16)
    out_ref[0] = cells
    level = first_level + pl.program_id(0)
    ids = lax.broadcasted_iota(jnp.int32, (OBS_CAP, width), 1) + level * width
    pick = jnp.where(ids == cell_ref[...], 1.0, 0.0).astype(jnp.bfloat16)
    seen = jnp.dot(pick, cells, preferred_element_type=jnp.float32)

    @pl.when(pl.program_id(0) == 0)
    def _():
        seen_ref[...] = seen

    @pl.when(pl.program_id(0) > 0)
    def _():
        seen_ref[...] += seen


def reaction(
    packed, in_t, bias_one, hid_t, bias_two, coef_half, rank_own, obs_cell, levels, first, earlier
):
    sources, part, per_source, tracers, slots = packed.shape
    members, _, hidden = coef_half.shape
    width = rank_own.shape[0]
    rows = members * tracers
    whole = lambda *dims: pl.BlockSpec(dims, lambda level: (0,) * len(dims))
    return pl.pallas_call(
        functools.partial(reaction_kernel, first),
        grid=(part,),
        in_specs=[
            pl.BlockSpec(
                (sources, 1, per_source, tracers, slots), lambda level: (0, level, 0, 0, 0)
            ),
            whole(hidden, tracers),
            whole(hidden, 1),
            whole(hidden, hidden),
            whole(hidden, 1),
            whole(members, tracers, hidden),
            whole(*rank_own.shape),
            whole(OBS_CAP, 1),
        ]
        + [pl.BlockSpec(memory_space=pl.ANY)] * len(earlier),
        out_specs=[
            pl.BlockSpec((1, width, rows), lambda level: (first + level, 0, 0)),
            whole(OBS_CAP, rows),
        ],
        out_shape=[
            jax.ShapeDtypeStruct((levels, width, rows), jnp.bfloat16),
            jax.ShapeDtypeStruct((OBS_CAP, rows), jnp.float32),
        ],
        input_output_aliases={8: 0} if earlier else {},
        scratch_shapes=[
            pltpu.VMEM((width, slots), jnp.bfloat16),
            pltpu.VMEM((rows, slots), jnp.bfloat16),
        ],
        compiler_params=pltpu.CompilerParams(vmem_limit_bytes=48 * 1024 * 1024),
        cost_estimate=pl.CostEstimate(
            flops=2 * part * rows * slots * (width + 2 * hidden + hidden * hidden // tracers),
            bytes_accessed=2 * part * rows * (slots + width),
            transcendentals=2 * part * members * slots * hidden,
        ),
        name="reaction",
    )(packed, in_t, bias_one, hid_t, bias_two, coef_half, rank_own, obs_cell, *earlier)


def sum_kernel(count, term_ref, out_ref, slots, send_sem, recv_sem):
    own = lax.axis_index("trc")
    peers = [lax.rem(own + step, count) for step in range(1, count)]
    barrier = pltpu.get_barrier_semaphore()
    for peer in peers:
        pl.semaphore_signal(
            barrier, inc=1, device_id={"trc": peer}, device_id_type=pl.DeviceIdType.MESH
        )
    pl.semaphore_wait(barrier, count - 1)
    copies = []
    for step, peer in enumerate(peers):
        copy = pltpu.make_async_remote_copy(
            src_ref=term_ref,
            dst_ref=slots.at[own],
            send_sem=send_sem.at[step],
            recv_sem=recv_sem.at[step],
            device_id={"trc": peer},
            device_id_type=pl.DeviceIdType.MESH,
        )
        copy.start()
        copies.append(copy)
    slots[own] = term_ref[...]
    for copy in copies:
        copy.wait()
    total = slots[0]
    for source in range(1, count):
        total = total + slots[source]
    out_ref[...] = total


def sum_over_blocks(terms):
    count = lax.axis_size("trc")
    return pl.pallas_call(
        functools.partial(sum_kernel, count),
        in_specs=[pl.BlockSpec(memory_space=pltpu.VMEM)],
        out_specs=pl.BlockSpec(memory_space=pltpu.VMEM),
        out_shape=jax.ShapeDtypeStruct(terms.shape, terms.dtype),
        scratch_shapes=[
            pltpu.VMEM((count,) + terms.shape, terms.dtype),
            pltpu.SemaphoreType.DMA((count - 1,)),
            pltpu.SemaphoreType.DMA((count - 1,)),
        ],
        compiler_params=pltpu.CompilerParams(
            collective_id=0, has_side_effects=True, vmem_limit_bytes=16 * 1024 * 1024
        ),
        name="block_sum",
    )(terms)


def solve_system(system, right_side):
    factor = jnp.linalg.cholesky(system)
    middle = lax.linalg.triangular_solve(factor, right_side, left_side=True, lower=True)
    return lax.linalg.triangular_solve(factor, middle, left_side=True, lower=True, transpose_a=True)


def shards(
    tracer_state,
    velocity,
    land_mask,
    in_weight,
    bias_one,
    hid_weight,
    bias_two,
    out_coef,
    obs_cell,
    obs_count,
    obs_value,
    obs_var,
    obs_noise,
):
    own_block = lax.axis_index("trc")
    group_index = lax.axis_index("ens")
    field_rows, levels, lat_rows, lon_count = tracer_state.shape
    members_here = out_coef.shape[0]
    tracers = in_weight.shape[0]
    group_rows = members_here * tracers
    highest = lax.Precision.HIGHEST
    wide = -(-lon_count // LANES) * LANES
    below = jnp.arange(lon_count)[:, None] < jnp.arange(lon_count)[None, :]
    before = jnp.dot(
        land_mask.astype(jnp.bfloat16), below.astype(jnp.bfloat16), preferred_element_type=jnp.float32
    )
    rank = jnp.where(land_mask > 0, before.astype(jnp.int32), -1)
    rank = jnp.pad(rank, ((0, 0), (0, wide - lon_count)), constant_values=-1)
    rank_own = lax.dynamic_slice_in_dim(rank, own_block, 1, 0)[:, :lon_count].T
    coef_half = out_coef.astype(jnp.bfloat16)
    in_t = in_weight.T * jnp.bfloat16(0.5)
    hid_t = hid_weight.T * jnp.bfloat16(0.5)
    half_one = bias_one[:, None] * 0.5
    half_two = bias_two[:, None] * 0.5
    flat_coef = out_coef.reshape(members_here, -1)
    coef_all = lax.all_gather(flat_coef, "ens", axis=0, tiled=True)
    obs_own = (obs_value[None] + obs_noise).reshape(obs_noise.shape[0], -1)
    cell_column = obs_cell.T
    part = levels // CHUNKS
    received = []
    for chunk in range(CHUNKS):
        if chunk == 1:
            ready = (rank, rank_own, coef_half, in_t, hid_t, half_one, half_two, cell_column, obs_own)
            ready = lax.optimization_barrier(ready)
            rank, rank_own, coef_half, in_t, hid_t, half_one, half_two, cell_column, obs_own = ready
        packed = transport_packed(tracer_state, velocity, land_mask, rank, tracers, chunk)
        received.append(lax.all_to_all(packed, "trc", split_axis=0, concat_axis=0, tiled=True))
    earlier = []
    predicted = 0.0
    for chunk in range(CHUNKS):
        cells, seen = reaction(
            received[chunk],
            in_t,
            half_one,
            hid_t,
            half_two,
            coef_half,
            rank_own,
            cell_column,
            levels,
            chunk * part,
            earlier,
        )
        earlier = [cells]
        predicted = predicted + seen
    new_cols = jnp.transpose(earlier[0], (2, 0, 1))[:, :, None]
    predicted_own = predicted.T.reshape(members_here, tracers, OBS_CAP)[:, :OBS_TR]
    predicted_own = predicted_own.astype(jnp.bfloat16)
    predicted_all = lax.all_gather(predicted_own, "ens", axis=0, tiled=True)
    member_total = predicted_all.shape[0]
    slot_ids = jnp.arange(OBS_CAP, dtype=jnp.int32)
    valid_slots = (slot_ids < obs_count[0]).astype(jnp.float32)
    weight = valid_slots[None, :] / obs_var[0]
    guessed = predicted_all.astype(jnp.float32).reshape(member_total, -1)
    anomaly = guessed - jnp.mean(guessed, axis=0)
    misfit = obs_own - guessed
    weighted = anomaly * weight.reshape(1, -1)
    terms = jnp.dot(
        weighted,
        jnp.concatenate([anomaly, misfit], axis=0).T,
        precision=highest,
        preferred_element_type=jnp.float32,
    )
    terms = sum_over_blocks(terms)
    gram, cross = terms[:, :member_total], terms[:, member_total:]
    system = (member_total - 1) * jnp.eye(member_total, dtype=jnp.float32) + gram
    mixing = solve_system(system, cross)
    first_member = group_index * members_here
    mixing_own = lax.dynamic_slice_in_dim(mixing, first_member, members_here, 1)
    summed = jnp.dot(
        mixing_own.T, coef_all, precision=highest, preferred_element_type=jnp.float32
    )
    new_coef = flat_coef + summed
    return (new_cols, new_coef.reshape(members_here, tracers, -1))


def solution(mesh):
    in_specs = (
        P(("ens", "trc"), None, None, None),
        P(),
        P(),
        P(),
        P(),
        P(),
        P(),
        P("ens", None, None),
        P("trc", None),
        P("trc"),
        P("trc", None, None),
        P("trc", None, None),
        P(None, "trc", None, None),
    )
    out_specs = (P("ens", None, "trc", None), P("ens", None, None))
    return jax.shard_map(shards, mesh=mesh, in_specs=in_specs, out_specs=out_specs, check_vma=False)
```
